32 devices in a mesh: groups: 2 (over x), dp: 16 (over z, y, core).
Axes of the slice: x: 2, y: 2, z: 4, core: 2. Of those that a mesh axis runs over, the one named last changes fastest.
Arguments:
- train_inputs: bfloat16 [8192, 4096], P(('groups', 'dp')), parts along dimension 0, may hold values from -4000 to 4000
- train_grads: bfloat16 [8192, 14336], P(('groups', 'dp')), parts along dimension 0, may hold values from -4000 to 4000
- proj_in: bfloat16 [64, 4096], replicated, may hold values from -0.09375 to 0.09375
- proj_out: bfloat16 [64, 14336], replicated, may hold values from -0.046875 to 0.046875
- query_grads: bfloat16 [256, 4096], P(('groups', 'dp')), parts along dimension 0, may hold values from -6 to 6
Outputs:
- scores: float32 [32, 128], P(('groups', 'dp')), parts along dimension 0
The draws below stay inside these ranges and needn't reach their ends.
There are 2 independent parts, one for each index of `groups`. The reference program is written for one: setup_inputs(seed, part) draws one part's arguments, and reference() takes and returns one part's arrays. A program takes and returns all parts, laid end to end along the dimension named above; an argument that names none is the same for every part. Nothing has to cross between parts.
All inputs are finite; a program needn't handle non-finite values.
Results may differ from the reference program's by a relative error of at most 0.0003.
Values may be sent and summed in bfloat16 or wider, within the bound.
No kernel may reach another device: no remote copies, remote signals or barrier semaphores. Data moves between devices by JAX's collectives and lax.ppermute only.
A program may use at most 128 MiB of HBM per device.

```python
import jax
import jax.numpy as jnp
from jax import lax

D = 4096
FF = 14336
R = 64
SEQ = 256
E_DEV = 1
TRAIN = 16
QUERIES = 128
TOKENS = 4096
N_DP = 16


def scaled_rows(key, base_draw, rise_rate, spike_weights):
    key_rows, key_cols, key_load, key_dirs = jax.random.split(key, 4)
    row_count, col_count = base_draw.shape
    position = jnp.arange(row_count, dtype=jnp.float32) / (row_count - 1)
    row_scale = jnp.exp(jax.random.uniform(key_rows, (row_count, 1)) * jnp.log(10.0)) * (1.0 + rise_rate * position)[:, None]
    col_scale = jnp.exp(jax.random.uniform(key_cols, (1, col_count)) * jnp.log(10.0))
    loadings = jax.random.normal(key_load, (row_count, 3))
    directions = jax.random.normal(key_dirs, (3, col_count))
    common = jnp.zeros((row_count, col_count), jnp.float32)
    for which in range(3):
        common = common + spike_weights[which] * loadings[:, which:which + 1] * directions[which:which + 1, :]
    return jnp.clip((base_draw + common) * row_scale * col_scale, -4000.0, 4000.0)


def draw_train_inputs(key, part):
    key = jax.random.fold_in(key, 11)
    key_base, key_scale = jax.random.split(key)
    base_draw = jax.random.normal(key_base, (TOKENS, D))
    values = scaled_rows(key_scale, base_draw, 2.0, (2.0, 1.0, 0.5))
    return values.astype(jnp.bfloat16)


def draw_train_grads(key, part):
    key = jax.random.fold_in(key, 12)
    key_base, key_scale = jax.random.split(key)
    base_draw = jax.random.normal(key_base, (TOKENS, FF))
    values = scaled_rows(key_scale, base_draw, 2.0, (2.0, 1.0, 0.5))
    return values.astype(jnp.bfloat16)


def shard_levels(stream_key, extent, cuts, least, high):
    factor_of, own = 1.0, jax.random.fold_in(stream_key, 6)
    for axis_at, shards_of in cuts:
        draws = jnp.exp(jax.random.uniform(jax.random.fold_in(own, axis_at), (shards_of,), jnp.float32, least / len(cuts), high / len(cuts)))
        factor_of = factor_of * jnp.repeat(draws, extent[axis_at] // shards_of).reshape([-1 if axis == axis_at else 1 for axis in range(len(extent))])
    return factor_of


def noise(key, shape, deviation, limit, cuts=(), kind=jnp.bfloat16):
    values = jax.random.normal(key, shape, jnp.float32) * deviation
    if len(cuts) > 0:
        values = shard_levels(key, shape, cuts, -0.22, 0.18) * values
    return jnp.clip(values, min=-limit, max=limit).astype(kind)


def setup_inputs(seed: int = 0, part: int = 0) -> dict:
    key_list = jax.random.split(jax.random.key(seed), 6)
    part_keys = jax.random.split(jax.random.fold_in(key_list[5], part), 6)
    train_inputs = draw_train_inputs(jax.random.fold_in(jax.random.fold_in(key_list[5], part), 71), part)
    train_grads = draw_train_grads(jax.random.fold_in(jax.random.fold_in(key_list[5], part), 71), part)
    proj_in = noise(key_list[2], (R, D), D ** -0.5, 0.09375)
    proj_out = noise(key_list[3], (R, FF), FF ** -0.5, 0.046875)
    query_grads = noise(part_keys[4], (QUERIES, R * R), 1.0, 6.0, ((0, 16),))
    return dict(train_inputs=train_inputs, train_grads=train_grads, proj_in=proj_in, proj_out=proj_out, query_grads=query_grads)


def project_rows(token_rows, weight):
    return lax.dot_general(token_rows.astype(jnp.float32), weight.astype(jnp.float32), (((1,), (1,)), ((), ())), preferred_element_type=jnp.float32)

def example_terms(inputs_block, grads_block, proj_in, proj_out, examples_count):
    inputs_low = project_rows(inputs_block, proj_in)
    grads_low = project_rows(grads_block, proj_out)
    rank_size = proj_in.shape[0]
    outer = jnp.einsum('esa,esb->eab', grads_low.reshape(examples_count, -1, rank_size), inputs_low.reshape(examples_count, -1, rank_size), precision=lax.Precision.HIGHEST)
    examples = outer.reshape(examples_count, rank_size * rank_size)
    moment_in = jnp.dot(inputs_low.T, inputs_low, precision=lax.Precision.HIGHEST)
    moment_out = jnp.dot(grads_low.T, grads_low, precision=lax.Precision.HIGHEST)
    return (examples, moment_in, moment_out)

def damped_inverse(moment):
    rank_size = moment.shape[0]
    identity = jnp.eye(rank_size, dtype=jnp.float32)
    damped = moment + 0.1 * jnp.trace(moment) / rank_size * identity
    factor = jnp.linalg.cholesky(damped)
    return jax.scipy.linalg.cho_solve((factor, True), identity)

def precondition(matrices, left_side, right_side):
    rank_size = left_side.shape[0]
    stacked = matrices.astype(jnp.float32).reshape(-1, rank_size, rank_size)
    result = jnp.einsum('ab,kbc,cd->kad', left_side, stacked, right_side, precision=lax.Precision.HIGHEST)
    return result.reshape(-1, rank_size * rank_size)

def reference(train_inputs, train_grads, proj_in, proj_out, query_grads):
    inputs_blocks = train_inputs.reshape(N_DP, E_DEV * SEQ, D)
    grads_blocks = train_grads.reshape(N_DP, E_DEV * SEQ, FF)

    def one_block(paired):
        return example_terms(paired[0], paired[1], proj_in, proj_out, E_DEV)
    examples, moment_in, moment_out = lax.map(one_block, (inputs_blocks, grads_blocks))
    examples = examples.reshape(TRAIN, R * R)
    moment_in = jnp.sum(moment_in, axis=0) / TOKENS
    moment_out = jnp.sum(moment_out, axis=0) / TOKENS
    inverse_in = damped_inverse(moment_in)
    inverse_out = damped_inverse(moment_out)
    queries_pre = precondition(query_grads, inverse_out, inverse_in)
    scores = jnp.dot(examples, queries_pre.T, precision=lax.Precision.HIGHEST)
    return scores / R
```

```python
import functools

import jax
import jax.numpy as jnp
from jax import lax
from jax.experimental import pallas as pl
from jax.experimental.pallas import tpu as pltpu
from jax.sharding import PartitionSpec as P

SEQ = 256
DAMPING = 0.1
CHUNK = 2048
MIB = 1024 * 1024
HIGHEST = lax.Precision.HIGHEST


def project_kernel(rank, plan, x_hbm, g_hbm, pin_hbm, pout_hbm, m_ref, e_ref, tok, wts, sems):
    copies = []
    for k, (which, start, size) in enumerate(plan):
        src, w_src = ((x_hbm, pin_hbm), (g_hbm, pout_hbm))[which]
        copies.append((
            pltpu.make_async_copy(w_src.at[:, pl.ds(start, size)], wts.at[k, :, pl.ds(0, size)], sems.at[0, k]),
            pltpu.make_async_copy(src.at[:, pl.ds(start, size)], tok.at[k, :, pl.ds(0, size)], sems.at[1, k]),
        ))
    for pair in copies:
        for copy in pair:
            copy.start()
    low = [None, None]
    for k, (which, start, size) in enumerate(plan):
        for copy in copies[k]:
            copy.wait()
        part = lax.dot_general(
            tok[k, :, :size], wts[k, :, :size], (((1,), (1,)), ((), ())), preferred_element_type=jnp.float32
        )
        low[which] = part if low[which] is None else low[which] + part
    both = jnp.concatenate(low, axis=1)
    gram = lax.dot_general(
        both, both, (((0,), (0,)), ((), ())), precision=HIGHEST, preferred_element_type=jnp.float32
    )
    lane = lax.broadcasted_iota(jnp.int32, (rank, 2 * rank), 1)
    m_ref[...] = jnp.where(lane < rank, gram[:rank], gram[rank:])
    e_ref[...] = gram[rank:]


def project(x, g, proj_in, proj_out):
    rank = proj_in.shape[0]
    plan = []
    for which, width in ((0, x.shape[1]), (1, g.shape[1])):
        for start in range(0, width, CHUNK):
            plan.append((which, start, min(CHUNK, width - start)))
    rows = x.shape[0]
    out = jax.ShapeDtypeStruct((rank, 2 * rank), jnp.float32)
    return pl.pallas_call(
        functools.partial(project_kernel, rank, plan),
        out_shape=(out, out),
        in_specs=[pl.BlockSpec(memory_space=pl.ANY)] * 4,
        out_specs=(pl.BlockSpec(memory_space=pltpu.VMEM),) * 2,
        scratch_shapes=[
            pltpu.VMEM((len(plan), rows, CHUNK), x.dtype),
            pltpu.VMEM((len(plan), rank, CHUNK), x.dtype),
            pltpu.SemaphoreType.DMA((2, len(plan))),
        ],
        compiler_params=pltpu.CompilerParams(vmem_limit_bytes=24 * MIB),
        cost_estimate=pl.CostEstimate(
            flops=2 * rows * rank * (x.shape[1] + g.shape[1]),
            bytes_accessed=2 * (rows + rank) * (x.shape[1] + g.shape[1]),
            transcendentals=0,
        ),
        name="project",
    )(x, g, proj_in, proj_out)


def newton_scales(rank):
    low = 2.0 / (2.0 + rank / DAMPING)
    scales = []
    while 1.0 - low > 0.02:
        image = low * (2.0 - low)
        scale = 2.0 / (1.0 + image)
        scales.append(scale)
        low = scale * image
    return scales


def dot(a, b):
    return jnp.dot(a, b, precision=HIGHEST, preferred_element_type=jnp.float32)


def score_kernel(rank, tokens, slots, m_ref, mr_ref, e_ref, qa_ref, qb_ref, o_ref, rows_scr, acc_scr):
    size = 2 * rank
    me = lax.axis_index("dp")
    total = (m_ref[...] + mr_ref[...]) * (1.0 / tokens)
    row = lax.broadcasted_iota(jnp.int32, (size, size), 0)
    col = lax.broadcasted_iota(jnp.int32, (size, size), 1)
    same = (row < rank) == (col < rank)
    eye = jnp.where(row == col, 1.0, 0.0)
    moment = jnp.where(same, jnp.concatenate([total, total], axis=0), 0.0)
    diagonal = jnp.where(row == col, moment, 0.0)
    by_col = jnp.sum(diagonal, axis=0, keepdims=True)
    half = lax.broadcasted_iota(jnp.int32, (1, size), 1) < rank
    trace_in = jnp.sum(jnp.where(half, by_col, 0.0), axis=1, keepdims=True)
    trace_out = jnp.sum(jnp.where(half, 0.0, by_col), axis=1, keepdims=True)
    damp = jnp.where(half, trace_in, trace_out) * (DAMPING / rank)
    a = moment + eye * damp
    first = (2.0 / (2.0 + rank / DAMPING)) / damp
    t = a * first
    x = eye * first
    for step, scale in enumerate(newton_scales(rank)):
        turn = 2.0 * eye - t
        x = scale * (x * turn if step == 0 else dot(x, turn))
        if step == 0:
            x = scale * (turn * first)
        t = scale * dot(t, turn)
    x = x + dot(x, eye - t)
    for _ in range(2):
        x = x + dot(x, eye - dot(a, x))
    pre = dot(dot(x[rank:, rank:], e_ref[:, :rank]), x[:rank, :])
    rows_scr[...] = pre
    even = rows_scr[pl.ds(0, rank // 2, stride=2), :]
    odd = rows_scr[pl.ds(1, rank // 2, stride=2), :]
    lane = lax.broadcasted_iota(jnp.int32, (rank // 2, size), 1)
    flat = jnp.where(lane < rank, even, pltpu.roll(odd, rank, 1))
    count = qa_ref.shape[0] // 16
    each = qa_ref.shape[0] * 2 // len(slots)
    for part, q_ref in enumerate((qa_ref, qb_ref)):
        for i in range(count):
            acc = jnp.zeros((16, size), jnp.float32)
            for j in range(rank // 2):
                block = q_ref[pl.ds(16 * i, 16), pl.ds(j * size, size)].astype(jnp.float32)
                acc = acc + block * flat[j:j + 1, :]
            for h in range(2):
                slot = slots[part * 2 * count + 2 * i + h]
                acc_scr[pl.ds(pl.multiple_of((me ^ slot) * each, each), each), :] = acc[8 * h:8 * h + 8]
    ones = jnp.ones((8, size), jnp.float32)
    sums = lax.dot_general(
        ones, acc_scr[...], (((1,), (1,)), ((), ())), precision=HIGHEST, preferred_element_type=jnp.float32
    )
    o_ref[...] = sums[0:1] * (1.0 / rank)


def body(n, train_inputs, train_grads, proj_in, proj_out, query_grads):
    rank = proj_in.shape[0]
    steps = [1 << b for b in range(n.bit_length() - 1)]

    def swap(value, step):
        return lax.ppermute(value, "dp", [(i, i ^ step) for i in range(n)])

    queries, slots = query_grads, [0]
    for step in reversed(steps):
        received = swap(queries, step)
        slots = slots + [slot ^ step for slot in slots]
        if step > 1:
            queries = jnp.concatenate([queries, received], axis=0)
    moment, example = project(train_inputs, train_grads, proj_in, proj_out)
    order = steps[:1] + steps[:0:-1]
    for step in order[:-1]:
        moment = moment + swap(moment, step)
    moment_far = swap(moment, order[-1])
    count = query_grads.shape[0] * n
    return pl.pallas_call(
        functools.partial(score_kernel, rank, train_inputs.shape[0] * n, slots),
        out_shape=jax.ShapeDtypeStruct((1, count), jnp.float32),
        in_specs=[pl.BlockSpec(memory_space=pltpu.VMEM)] * 5,
        out_specs=pl.BlockSpec(memory_space=pltpu.VMEM),
        scratch_shapes=[
            pltpu.VMEM((rank, 2 * rank), jnp.float32),
            pltpu.VMEM((count, 2 * rank), jnp.float32),
        ],
        compiler_params=pltpu.CompilerParams(vmem_limit_bytes=24 * MIB),
        name="score",
    )(moment, moment_far, example, queries, received)


def solution(mesh):
    n = mesh.shape["dp"]
    return jax.shard_map(
        functools.partial(body, n),
        mesh=mesh,
        in_specs=(
            P(("groups", "dp"), None),
            P(("groups", "dp"), None),
            P(),
            P(),
            P(("groups", "dp"), None),
        ),
        out_specs=P(("groups", "dp"), None),
        check_vma=False,
    )
```

```python
import functools
import math

import jax
import jax.numpy as jnp
from jax import lax
from jax.experimental import pallas as pl
from jax.experimental.pallas import tpu as pltpu
from jax.sharding import PartitionSpec as P

SEQ = 256
DAMPING = 0.1
CHUNK = 2048
PROJECT_MIB = 53.6
MIB = 1024 * 1024
HIGHEST = lax.Precision.HIGHEST


def project_kernel(rank, chunk, x_hbm, g_hbm, pin_hbm, pout_hbm, m_ref, e_ref, xt, gt, wi, wo, sems):
    x_count, g_count = xt.shape[0], gt.shape[0]

    def copies(src, dst, w_src, w_dst, base, k):
        part = pl.ds(pl.multiple_of(k * chunk, chunk), chunk)
        return (
            pltpu.make_async_copy(w_src.at[:, part], w_dst.at[k], sems.at[0, base + k]),
            pltpu.make_async_copy(src.at[:, part], dst.at[k], sems.at[1, base + k]),
        )

    x_copies = functools.partial(copies, x_hbm, xt, pin_hbm, wi, 0)
    g_copies = functools.partial(copies, g_hbm, gt, pout_hbm, wo, x_count)

    def start(make, k, carry):
        for copy in make(k):
            copy.start()
        return carry

    lax.fori_loop(0, x_count, functools.partial(start, x_copies), 0)
    lax.fori_loop(0, g_count, functools.partial(start, g_copies), 0)

    def multiply(make, tokens, weights, k, total):
        for copy in make(k):
            copy.wait()
        return total + lax.dot_general(
            weights[k], tokens[k], (((1,), (1,)), ((), ())), preferred_element_type=jnp.float32
        )

    zero = jnp.zeros((rank, xt.shape[1]), jnp.float32)
    x_low = lax.fori_loop(0, x_count, functools.partial(multiply, x_copies, xt, wi), zero)
    g_low = lax.fori_loop(0, g_count, functools.partial(multiply, g_copies, gt, wo), zero)
    a0, a1, a2 = split(jnp.concatenate([x_low, g_low], axis=0), 3)
    gram = lax.dot_general(
        jnp.concatenate([a0, a0, a1, a1, a0, a2], axis=1),
        jnp.concatenate([a0, a1, a0, a1, a2, a0], axis=1),
        (((1,), (1,)), ((), ())),
        preferred_element_type=jnp.float32,
    )
    lane = lax.broadcasted_iota(jnp.int32, (rank, 2 * rank), 1)
    m_ref[...] = jnp.where(lane < rank, gram[:rank], gram[rank:])
    e_ref[...] = gram[rank:]


def project(x, g, proj_in, proj_out):
    rank, rows = proj_in.shape[0], x.shape[0]
    chunk = math.gcd(math.gcd(x.shape[1], g.shape[1]), CHUNK)
    x_count, g_count = x.shape[1] // chunk, g.shape[1] // chunk
    out = jax.ShapeDtypeStruct((rank, 2 * rank), jnp.float32)
    return pl.pallas_call(
        functools.partial(project_kernel, rank, chunk),
        out_shape=(out, out),
        in_specs=[pl.BlockSpec(memory_space=pltpu.HBM)] * 4,
        out_specs=(pl.BlockSpec(memory_space=pltpu.VMEM),) * 2,
        scratch_shapes=[
            pltpu.VMEM((x_count, rows, chunk), x.dtype),
            pltpu.VMEM((g_count, rows, chunk), x.dtype),
            pltpu.VMEM((x_count, rank, chunk), x.dtype),
            pltpu.VMEM((g_count, rank, chunk), x.dtype),
            pltpu.SemaphoreType.DMA((2, x_count + g_count)),
        ],
        compiler_params=pltpu.CompilerParams(vmem_limit_bytes=int(PROJECT_MIB * MIB)),
        cost_estimate=pl.CostEstimate(
            flops=2 * rows * rank * (x.shape[1] + g.shape[1]),
            bytes_accessed=2 * (rows + rank) * (x.shape[1] + g.shape[1]),
            transcendentals=0,
        ),
        name="project",
    )(x, g, proj_in, proj_out)


def newton_scales(rank):
    low = 2.0 / (2.0 + rank / DAMPING)
    scales = []
    while 1.0 - low > 0.02:
        image = low * (2.0 - low)
        scale = 2.0 / (1.0 + image)
        scales.append(scale)
        low = scale * image
    return scales


def split(a, terms):
    parts = []
    for _ in range(terms):
        part = a.astype(jnp.bfloat16)
        parts.append(part)
        a = a - part.astype(jnp.float32)
    return parts


def dot(a, b):
    (a0, a1, a2), (b0, b1, b2) = split(a, 3), split(b, 3)
    left = jnp.concatenate([a0, a0, a1, a1, a0, a2], axis=1)
    right = jnp.concatenate([b0, b1, b0, b1, b2, b0], axis=0)
    return jnp.dot(left, right, preferred_element_type=jnp.float32)


def coarse_dot(a, b):
    (a0, a1), (b0, b1) = split(a, 2), split(b, 2)
    left = jnp.concatenate([a0, a1, a0], axis=1)
    right = jnp.concatenate([b0, b0, b1], axis=0)
    return jnp.dot(left, right, preferred_element_type=jnp.float32)


def invert_kernel(rank, tokens, m_ref, mr_ref, e_ref, flat_ref, rows_scr):
    size = 2 * rank
    total = (m_ref[...] + mr_ref[...]) * (1.0 / tokens)
    row = lax.broadcasted_iota(jnp.int32, (size, size), 0)
    col = lax.broadcasted_iota(jnp.int32, (size, size), 1)
    same = (row < rank) == (col < rank)
    eye = jnp.where(row == col, 1.0, 0.0)
    moment = jnp.where(same, jnp.concatenate([total, total], axis=0), 0.0)
    diagonal = jnp.where(row == col, moment, 0.0)
    by_col = jnp.sum(diagonal, axis=0, keepdims=True)
    half = lax.broadcasted_iota(jnp.int32, (1, size), 1) < rank
    trace_in = jnp.sum(jnp.where(half, by_col, 0.0), axis=1, keepdims=True)
    trace_out = jnp.sum(jnp.where(half, 0.0, by_col), axis=1, keepdims=True)
    damp = jnp.where(half, trace_in, trace_out) * (DAMPING / rank)
    a = moment + eye * damp
    first = (2.0 / (2.0 + rank / DAMPING)) / damp
    t = a * first
    for step, scale in enumerate(newton_scales(rank)):
        turn = scale * (2.0 * eye - t)
        if step == 0:
            x, t = turn * first, coarse_dot(t, turn)
        else:
            both = coarse_dot(jnp.concatenate([x, t], axis=0), turn)
            x, t = both[:size], both[size:]
    x = x + coarse_dot(x, eye - t)
    for _ in range(2):
        x = x + coarse_dot(x, eye - dot(a, x))
    pre = dot(dot(x[rank:, rank:], e_ref[:, :rank]), x[:rank, :])
    rows_scr[...] = pre
    even = rows_scr[pl.ds(0, rank // 2, stride=2), :]
    odd = rows_scr[pl.ds(1, rank // 2, stride=2), :]
    lane = lax.broadcasted_iota(jnp.int32, (rank // 2, size), 1)
    flat_ref[...] = jnp.where(lane < rank, even, pltpu.roll(odd, rank, 1))


def score_kernel(rank, slots, flat_ref, qa_ref, qb_ref, o_ref, acc_scr):
    size = 2 * rank
    me = lax.axis_index("dp")
    count = qa_ref.shape[0] // 16
    each = qa_ref.shape[0] * 2 // len(slots)
    for part, q_ref in enumerate((qa_ref, qb_ref)):
        for i in range(count):
            acc = jnp.zeros((16, size), jnp.float32)
            for j in range(rank // 2):
                block = q_ref[pl.ds(16 * i, 16), pl.ds(j * size, size)].astype(jnp.float32)
                acc = acc + block * flat_ref[j:j + 1, :]
            for h in range(2):
                slot = slots[part * 2 * count + 2 * i + h]
                acc_scr[pl.ds(pl.multiple_of((me ^ slot) * each, each), each), :] = acc[8 * h:8 * h + 8]
    ones = jnp.ones((8, size), jnp.float32)
    sums = lax.dot_general(
        ones, acc_scr[...], (((1,), (1,)), ((), ())), precision=HIGHEST, preferred_element_type=jnp.float32
    )
    o_ref[...] = sums[0:1] * (1.0 / rank)


def body(n, train_inputs, train_grads, proj_in, proj_out, query_grads):
    rank = proj_in.shape[0]
    steps = [1 << b for b in range(n.bit_length() - 1)]

    def swap(value, step):
        return lax.ppermute(value, "dp", [(i, i ^ step) for i in range(n)])

    moment, example = project(train_inputs, train_grads, proj_in, proj_out)
    far, near = steps[-1], steps[-2]
    slots = [0, far, near, far ^ near]
    pieces = [query_grads] + [swap(query_grads, step) for step in slots[1:]]
    moment, pieces = lax.optimization_barrier((moment, pieces))
    queries = jnp.concatenate(pieces[:2], axis=0)
    received = jnp.concatenate(pieces[2:], axis=0)
    for step in steps[-3::-1]:
        queries = jnp.concatenate([queries, received], axis=0)
        received = swap(queries, step)
        slots = slots + [slot ^ step for slot in slots]
    order = steps[:2] + steps[:1:-1]
    for step in order[:-1]:
        moment = moment + swap(moment, step)
    moment_far = swap(moment, order[-1])
    flat = pl.pallas_call(
        functools.partial(invert_kernel, rank, train_inputs.shape[0] * n),
        out_shape=jax.ShapeDtypeStruct((rank // 2, 2 * rank), jnp.float32),
        in_specs=[pl.BlockSpec(memory_space=pltpu.VMEM)] * 3,
        out_specs=pl.BlockSpec(memory_space=pltpu.VMEM),
        scratch_shapes=[pltpu.VMEM((rank, 2 * rank), jnp.float32)],
        compiler_params=pltpu.CompilerParams(vmem_limit_bytes=8 * MIB),
        cost_estimate=pl.CostEstimate(flops=10 ** 11, bytes_accessed=10 ** 5, transcendentals=0),
        name="invert",
    )(moment, moment_far, example)
    count = query_grads.shape[0] * n
    return pl.pallas_call(
        functools.partial(score_kernel, rank, slots),
        out_shape=jax.ShapeDtypeStruct((1, count), jnp.float32),
        in_specs=[pl.BlockSpec(memory_space=pltpu.VMEM)] * 3,
        out_specs=pl.BlockSpec(memory_space=pltpu.VMEM),
        scratch_shapes=[pltpu.VMEM((count, 2 * rank), jnp.float32)],
        compiler_params=pltpu.CompilerParams(vmem_limit_bytes=24 * MIB),
        name="score",
    )(flat, queries, received)


def solution(mesh):
    n = mesh.shape["dp"]
    return jax.shard_map(
        functools.partial(body, n),
        mesh=mesh,
        in_specs=(
            P(("groups", "dp"), None),
            P(("groups", "dp"), None),
            P(),
            P(),
            P(("groups", "dp"), None),
        ),
        out_specs=P(("groups", "dp"), None),
        check_vma=False,
    )
```

```python
import functools
import math

import jax
import jax.numpy as jnp
from jax import lax
from jax.experimental import pallas as pl
from jax.experimental.pallas import tpu as pltpu
from jax.sharding import PartitionSpec as P

SEQ = 256
DAMPING = 0.1
CHUNK = 2048
PROJECT_MIB = 53.6
MIB = 1024 * 1024
HIGHEST = lax.Precision.HIGHEST


def project_kernel(rank, chunk, x_hbm, g_hbm, pin_hbm, pout_hbm, m_ref, e_ref, xt, gt, wi, wo, sems):
    x_count, g_count = xt.shape[0], gt.shape[0]

    def copies(src, dst, w_src, w_dst, base, k):
        part = pl.ds(pl.multiple_of(k * chunk, chunk), chunk)
        return (
            pltpu.make_async_copy(w_src.at[:, part], w_dst.at[k], sems.at[0, base + k]),
            pltpu.make_async_copy(src.at[:, part], dst.at[k], sems.at[1, base + k]),
        )

    x_copies = functools.partial(copies, x_hbm, xt, pin_hbm, wi, 0)
    g_copies = functools.partial(copies, g_hbm, gt, pout_hbm, wo, x_count)

    def start(make, k, carry):
        for copy in make(k):
            copy.start()
        return carry

    lax.fori_loop(0, x_count, functools.partial(start, x_copies), 0)
    lax.fori_loop(0, g_count, functools.partial(start, g_copies), 0)

    def multiply(make, tokens, weights, k, total):
        for copy in make(k):
            copy.wait()
        return total + lax.dot_general(
            weights[k], tokens[k], (((1,), (1,)), ((), ())), preferred_element_type=jnp.float32
        )

    zero = jnp.zeros((rank, xt.shape[1]), jnp.float32)
    x_low = lax.fori_loop(0, x_count, functools.partial(multiply, x_copies, xt, wi), zero)
    g_low = lax.fori_loop(0, g_count, functools.partial(multiply, g_copies, gt, wo), zero)
    a0, a1, a2 = split(jnp.concatenate([x_low, g_low], axis=0), 3)
    gram = lax.dot_general(
        jnp.concatenate([a0, a0, a1, a1, a0, a2], axis=1),
        jnp.concatenate([a0, a1, a0, a1, a2, a0], axis=1),
        (((1,), (1,)), ((), ())),
        preferred_element_type=jnp.float32,
    )
    lane = lax.broadcasted_iota(jnp.int32, (rank, 2 * rank), 1)
    m_ref[...] = jnp.where(lane < rank, gram[:rank], gram[rank:])
    e_ref[...] = gram[rank:]


def project(x, g, proj_in, proj_out):
    rank, rows = proj_in.shape[0], x.shape[0]
    chunk = math.gcd(math.gcd(x.shape[1], g.shape[1]), CHUNK)
    x_count, g_count = x.shape[1] // chunk, g.shape[1] // chunk
    out = jax.ShapeDtypeStruct((rank, 2 * rank), jnp.float32)
    return pl.pallas_call(
        functools.partial(project_kernel, rank, chunk),
        out_shape=(out, out),
        in_specs=[pl.BlockSpec(memory_space=pltpu.HBM)] * 4,
        out_specs=(pl.BlockSpec(memory_space=pltpu.VMEM),) * 2,
        scratch_shapes=[
            pltpu.VMEM((x_count, rows, chunk), x.dtype),
            pltpu.VMEM((g_count, rows, chunk), x.dtype),
            pltpu.VMEM((x_count, rank, chunk), x.dtype),
            pltpu.VMEM((g_count, rank, chunk), x.dtype),
            pltpu.SemaphoreType.DMA((2, x_count + g_count)),
        ],
        compiler_params=pltpu.CompilerParams(vmem_limit_bytes=int(PROJECT_MIB * MIB)),
        cost_estimate=pl.CostEstimate(
            flops=2 * rows * rank * (x.shape[1] + g.shape[1]),
            bytes_accessed=2 * (rows + rank) * (x.shape[1] + g.shape[1]),
            transcendentals=0,
        ),
        name="project",
    )(x, g, proj_in, proj_out)


def newton_scales(rank):
    low = 2.0 / (2.0 + rank / DAMPING)
    scales = []
    while 1.0 - low > 0.02:
        image = low * (2.0 - low)
        scale = 2.0 / (1.0 + image)
        scales.append(scale)
        low = scale * image
    return scales


def split(a, terms):
    parts = []
    for _ in range(terms):
        part = a.astype(jnp.bfloat16)
        parts.append(part)
        a = a - part.astype(jnp.float32)
    return parts


def dot(a, b):
    (a0, a1, a2), (b0, b1, b2) = split(a, 3), split(b, 3)
    left = jnp.concatenate([a0, a0, a1, a1, a0, a2], axis=1)
    right = jnp.concatenate([b0, b1, b0, b1, b2, b0], axis=0)
    return jnp.dot(left, right, preferred_element_type=jnp.float32)


def coarse_dot(a, b):
    (a0, a1), (b0, b1) = split(a, 2), split(b, 2)
    left = jnp.concatenate([a0, a1, a0], axis=1)
    right = jnp.concatenate([b0, b0, b1], axis=0)
    return jnp.dot(left, right, preferred_element_type=jnp.float32)


def invert_kernel(rank, tokens, m_ref, mr_ref, e_ref, flat_ref, rows_scr):
    size = 2 * rank
    low = lax.broadcasted_iota(jnp.int32, (rank, size), 1) < rank
    row = lax.broadcasted_iota(jnp.int32, (rank, size), 0)
    col = lax.broadcasted_iota(jnp.int32, (rank, size), 1)
    on_diagonal = jnp.where(low, col, col - rank) == row
    eye = jnp.where(on_diagonal, 1.0, 0.0)

    def blocks(pair):
        zero = jnp.zeros_like(pair)
        return jnp.concatenate([jnp.where(low, pair, zero), jnp.where(low, zero, pair)], axis=0)

    moment = (m_ref[...] + mr_ref[...]) * (1.0 / tokens)
    by_col = jnp.sum(jnp.where(on_diagonal, moment, 0.0), axis=0, keepdims=True)
    half = lax.broadcasted_iota(jnp.int32, (1, size), 1) < rank
    trace_in = jnp.sum(jnp.where(half, by_col, 0.0), axis=1, keepdims=True)
    trace_out = jnp.sum(jnp.where(half, 0.0, by_col), axis=1, keepdims=True)
    damp = jnp.where(half, trace_in, trace_out) * (DAMPING / rank)
    a = moment + eye * damp
    first = (2.0 / (2.0 + rank / DAMPING)) / damp
    t = a * first
    for step, scale in enumerate(newton_scales(rank)):
        turn = scale * (2.0 * eye - t)
        if step == 0:
            x, t = turn * first, coarse_dot(t, blocks(turn))
        else:
            both = coarse_dot(jnp.concatenate([x, t], axis=0), blocks(turn))
            x, t = both[:rank], both[rank:]
    x = x + coarse_dot(x, blocks(eye - t))
    for _ in range(2):
        x = x + coarse_dot(x, blocks(eye - dot(a, blocks(x))))
    inverses = blocks(x)
    example = jnp.where(low, e_ref[...], 0.0)
    left = dot(inverses[rank:], jnp.concatenate([jnp.zeros_like(example), example], axis=0))
    rows_scr[...] = dot(left, jnp.concatenate([inverses[:rank], jnp.zeros_like(example)], axis=0))
    even = rows_scr[pl.ds(0, rank // 2, stride=2), :]
    odd = rows_scr[pl.ds(1, rank // 2, stride=2), :]
    lane = lax.broadcasted_iota(jnp.int32, (rank // 2, size), 1)
    flat_ref[...] = jnp.where(lane < rank, even, pltpu.roll(odd, rank, 1))


def score_kernel(rank, slots, flat_ref, qa_ref, qb_ref, o_ref, acc_scr):
    size = 2 * rank
    me = lax.axis_index("dp")
    count = qa_ref.shape[0] // 16
    each = qa_ref.shape[0] * 2 // len(slots)
    for part, q_ref in enumerate((qa_ref, qb_ref)):
        for i in range(count):
            acc = jnp.zeros((16, size), jnp.float32)
            for j in range(rank // 2):
                block = q_ref[pl.ds(16 * i, 16), pl.ds(j * size, size)].astype(jnp.float32)
                acc = acc + block * flat_ref[j:j + 1, :]
            for h in range(2):
                slot = slots[part * 2 * count + 2 * i + h]
                acc_scr[pl.ds(pl.multiple_of((me ^ slot) * each, each), each), :] = acc[8 * h:8 * h + 8]
    ones = jnp.ones((8, size), jnp.float32)
    sums = lax.dot_general(
        ones, acc_scr[...], (((1,), (1,)), ((), ())), precision=HIGHEST, preferred_element_type=jnp.float32
    )
    o_ref[...] = sums[0:1] * (1.0 / rank)


def body(n, train_inputs, train_grads, proj_in, proj_out, query_grads):
    rank = proj_in.shape[0]
    steps = [1 << b for b in range(n.bit_length() - 1)]

    def swap(value, step):
        return lax.ppermute(value, "dp", [(i, i ^ step) for i in range(n)])

    moment, example = project(train_inputs, train_grads, proj_in, proj_out)
    far, near = steps[-1], steps[-2]
    slots = [0, far, near, far ^ near]
    pieces = [query_grads] + [swap(query_grads, step) for step in slots[1:]]
    moment, early = lax.optimization_barrier((moment, pieces[:2]))
    sums, order = [moment], steps[:2] + steps[:1:-1]
    for step in order[:-1]:
        sums.append(sums[-1] + swap(sums[-1], step))
    moment, moment_far = sums[-1], swap(sums[-1], order[-1])

    def beside(k, value):
        return lax.optimization_barrier((sums[k], value))[1]

    pieces = early + [beside(1, piece) for piece in pieces[2:]]
    queries = jnp.concatenate(pieces[:2], axis=0)
    received = jnp.concatenate(pieces[2:], axis=0)
    for step in steps[-3::-1]:
        queries = jnp.concatenate([queries, received], axis=0)
        received = swap(beside(1, queries) if step == steps[1] else queries, step)
        slots = slots + [slot ^ step for slot in slots]
    flat = pl.pallas_call(
        functools.partial(invert_kernel, rank, train_inputs.shape[0] * n),
        out_shape=jax.ShapeDtypeStruct((rank // 2, 2 * rank), jnp.float32),
        in_specs=[pl.BlockSpec(memory_space=pltpu.VMEM)] * 3,
        out_specs=pl.BlockSpec(memory_space=pltpu.VMEM),
        scratch_shapes=[pltpu.VMEM((rank, 2 * rank), jnp.float32)],
        compiler_params=pltpu.CompilerParams(vmem_limit_bytes=8 * MIB),
        cost_estimate=pl.CostEstimate(flops=10 ** 11, bytes_accessed=10 ** 5, transcendentals=0),
        name="invert",
    )(moment, moment_far, example)
    count = query_grads.shape[0] * n
    return pl.pallas_call(
        functools.partial(score_kernel, rank, slots),
        out_shape=jax.ShapeDtypeStruct((1, count), jnp.float32),
        in_specs=[pl.BlockSpec(memory_space=pltpu.VMEM)] * 3,
        out_specs=pl.BlockSpec(memory_space=pltpu.VMEM),
        scratch_shapes=[pltpu.VMEM((count, 2 * rank), jnp.float32)],
        compiler_params=pltpu.CompilerParams(vmem_limit_bytes=24 * MIB),
        name="score",
    )(flat, queries, received)


def solution(mesh):
    n = mesh.shape["dp"]
    return jax.shard_map(
        functools.partial(body, n),
        mesh=mesh,
        in_specs=(
            P(("groups", "dp"), None),
            P(("groups", "dp"), None),
            P(),
            P(),
            P(("groups", "dp"), None),
        ),
        out_specs=P(("groups", "dp"), None),
        check_vma=False,
    )
```

```python
import functools
import math

import jax
import jax.numpy as jnp
from jax import lax
from jax.experimental import pallas as pl
from jax.experimental.pallas import tpu as pltpu
from jax.sharding import PartitionSpec as P

SEQ = 256
DAMPING = 0.1
CHUNK = 2048
PROJECT_MIB = 53.6
MIB = 1024 * 1024
HIGHEST = lax.Precision.HIGHEST


def project_kernel(rank, chunk, x_hbm, g_hbm, pin_hbm, pout_hbm, m_ref, e_ref, xt, gt, wi, wo, sems):
    x_count, g_count = xt.shape[0], gt.shape[0]

    def copies(src, dst, w_src, w_dst, base, k):
        part = pl.ds(pl.multiple_of(k * chunk, chunk), chunk)
        return (
            pltpu.make_async_copy(w_src.at[:, part], w_dst.at[k], sems.at[0, base + k]),
            pltpu.make_async_copy(src.at[:, part], dst.at[k], sems.at[1, base + k]),
        )

    x_copies = functools.partial(copies, x_hbm, xt, pin_hbm, wi, 0)
    g_copies = functools.partial(copies, g_hbm, gt, pout_hbm, wo, x_count)

    def start(make, k, carry):
        for copy in make(k):
            copy.start()
        return carry

    lax.fori_loop(0, x_count, functools.partial(start, x_copies), 0)
    lax.fori_loop(0, g_count, functools.partial(start, g_copies), 0)

    def multiply(make, tokens, weights, k, total):
        for copy in make(k):
            copy.wait()
        return total + lax.dot_general(
            weights[k], tokens[k], (((1,), (1,)), ((), ())), preferred_element_type=jnp.float32
        )

    zero = jnp.zeros((rank, xt.shape[1]), jnp.float32)
    x_low = lax.fori_loop(0, x_count, functools.partial(multiply, x_copies, xt, wi), zero)
    g_low = lax.fori_loop(0, g_count, functools.partial(multiply, g_copies, gt, wo), zero)
    a0, a1, a2 = split(jnp.concatenate([x_low, g_low], axis=0), 3)
    gram = lax.dot_general(
        jnp.concatenate([a0, a0, a1, a1, a0, a2], axis=1),
        jnp.concatenate([a0, a1, a0, a1, a2, a0], axis=1),
        (((1,), (1,)), ((), ())),
        preferred_element_type=jnp.float32,
    )
    lane = lax.broadcasted_iota(jnp.int32, (rank, 2 * rank), 1)
    m_ref[...] = jnp.where(lane < rank, gram[:rank], gram[rank:])
    e_ref[...] = gram[rank:]


def project(x, g, proj_in, proj_out):
    rank, rows = proj_in.shape[0], x.shape[0]
    chunk = math.gcd(math.gcd(x.shape[1], g.shape[1]), CHUNK)
    x_count, g_count = x.shape[1] // chunk, g.shape[1] // chunk
    out = jax.ShapeDtypeStruct((rank, 2 * rank), jnp.float32)
    return pl.pallas_call(
        functools.partial(project_kernel, rank, chunk),
        out_shape=(out, out),
        in_specs=[pl.BlockSpec(memory_space=pltpu.HBM)] * 4,
        out_specs=(pl.BlockSpec(memory_space=pltpu.VMEM),) * 2,
        scratch_shapes=[
            pltpu.VMEM((x_count, rows, chunk), x.dtype),
            pltpu.VMEM((g_count, rows, chunk), x.dtype),
            pltpu.VMEM((x_count, rank, chunk), x.dtype),
            pltpu.VMEM((g_count, rank, chunk), x.dtype),
            pltpu.SemaphoreType.DMA((2, x_count + g_count)),
        ],
        compiler_params=pltpu.CompilerParams(vmem_limit_bytes=int(PROJECT_MIB * MIB)),
        cost_estimate=pl.CostEstimate(
            flops=2 * rows * rank * (x.shape[1] + g.shape[1]),
            bytes_accessed=2 * (rows + rank) * (x.shape[1] + g.shape[1]),
            transcendentals=0,
        ),
        name="project",
    )(x, g, proj_in, proj_out)


def newton_scales(rank):
    low = 2.0 / (2.0 + rank / DAMPING)
    scales = []
    while 1.0 - low > 0.02:
        image = low * (2.0 - low)
        scale = 2.0 / (1.0 + image)
        scales.append(scale)
        low = scale * image
    return scales


def split(a, terms):
    parts = []
    for _ in range(terms):
        part = a.astype(jnp.bfloat16)
        parts.append(part)
        a = a - part.astype(jnp.float32)
    return parts


def dot(a, b):
    (a0, a1, a2), (b0, b1, b2) = split(a, 3), split(b, 3)
    left = jnp.concatenate([a0, a0, a1, a1, a0, a2], axis=1)
    right = jnp.concatenate([b0, b1, b0, b1, b2, b0], axis=0)
    return jnp.dot(left, right, preferred_element_type=jnp.float32)


def coarse_dot(a, b):
    (a0, a1), (b0, b1) = split(a, 2), split(b, 2)
    left = jnp.concatenate([a0, a1, a0], axis=1)
    right = jnp.concatenate([b0, b0, b1], axis=0)
    return jnp.dot(left, right, preferred_element_type=jnp.float32)


def invert_kernel(rank, tokens, m_ref, mr_ref, e_ref, flat_ref, rows_scr):
    size = 2 * rank
    low = lax.broadcasted_iota(jnp.int32, (rank, size), 1) < rank
    row = lax.broadcasted_iota(jnp.int32, (rank, size), 0)
    col = lax.broadcasted_iota(jnp.int32, (rank, size), 1)
    on_diagonal = jnp.where(low, col, col - rank) == row
    eye = jnp.where(on_diagonal, 1.0, 0.0)

    def blocks(pair):
        zero = jnp.zeros_like(pair)
        return jnp.concatenate([jnp.where(low, pair, zero), jnp.where(low, zero, pair)], axis=0)

    moment = (m_ref[...] + mr_ref[...]) * (1.0 / tokens)
    by_col = jnp.sum(jnp.where(on_diagonal, moment, 0.0), axis=0, keepdims=True)
    half = lax.broadcasted_iota(jnp.int32, (1, size), 1) < rank
    trace_in = jnp.sum(jnp.where(half, by_col, 0.0), axis=1, keepdims=True)
    trace_out = jnp.sum(jnp.where(half, 0.0, by_col), axis=1, keepdims=True)
    damp = jnp.where(half, trace_in, trace_out) * (DAMPING / rank)
    a = moment + eye * damp
    first = (2.0 / (2.0 + rank / DAMPING)) / damp
    t = a * first
    for step, scale in enumerate(newton_scales(rank)):
        turn = scale * (2.0 * eye - t)
        if step == 0:
            x, t = turn * first, coarse_dot(t, blocks(turn))
        else:
            both = coarse_dot(jnp.concatenate([x, t], axis=0), blocks(turn))
            x, t = both[:rank], both[rank:]
    for _ in range(2):
        x = x + coarse_dot(x, blocks(eye - dot(a, blocks(x))))
    inverses = blocks(x)
    example = jnp.where(low, e_ref[...], 0.0)
    left = dot(inverses[rank:], jnp.concatenate([jnp.zeros_like(example), example], axis=0))
    rows_scr[...] = dot(left, jnp.concatenate([inverses[:rank], jnp.zeros_like(example)], axis=0))
    even = rows_scr[pl.ds(0, rank // 2, stride=2), :]
    odd = rows_scr[pl.ds(1, rank // 2, stride=2), :]
    lane = lax.broadcasted_iota(jnp.int32, (rank // 2, size), 1)
    flat_ref[...] = jnp.where(lane < rank, even, pltpu.roll(odd, rank, 1))


def score_kernel(rank, slots, flat_ref, qa_ref, qb_ref, o_ref, acc_scr):
    size = 2 * rank
    me = lax.axis_index("dp")
    count = qa_ref.shape[0] // 16
    each = qa_ref.shape[0] * 2 // len(slots)
    for part, q_ref in enumerate((qa_ref, qb_ref)):
        for i in range(count):
            acc = jnp.zeros((16, size), jnp.float32)
            for j in range(rank // 2):
                block = q_ref[pl.ds(16 * i, 16), pl.ds(j * size, size)].astype(jnp.float32)
                acc = acc + block * flat_ref[j:j + 1, :]
            for h in range(2):
                slot = slots[part * 2 * count + 2 * i + h]
                acc_scr[pl.ds(pl.multiple_of((me ^ slot) * each, each), each), :] = acc[8 * h:8 * h + 8]
    ones = jnp.ones((8, size), jnp.bfloat16)
    sums = sum(
        lax.dot_general(ones, part, (((1,), (1,)), ((), ())), preferred_element_type=jnp.float32)
        for part in split(acc_scr[...], 3)
    )
    o_ref[...] = sums[0:1] * (1.0 / rank)


def body(n, train_inputs, train_grads, proj_in, proj_out, query_grads):
    rank = proj_in.shape[0]
    steps = [1 << b for b in range(n.bit_length() - 1)]

    def swap(value, step):
        return lax.ppermute(value, "dp", [(i, i ^ step) for i in range(n)])

    moment, example = project(train_inputs, train_grads, proj_in, proj_out)
    far, near = steps[-1], steps[-2]
    slots = [0, far, near, far ^ near]
    before = {i: swap(query_grads, slots[i]) for i in (1, 3)}
    first = 1
    moment, before[first], own = lax.optimization_barrier((moment, before[first], query_grads))
    sums, order = [moment], steps
    for step in order[:-1]:
        sums.append(sums[-1] + swap(sums[-1], step))
    moment, moment_far = sums[-1], swap(sums[-1], order[-1])

    def beside(k, value):
        return value if k is None else lax.optimization_barrier((sums[k], value))[1]

    for i, k in ((2, 0),):
        before[i] = swap(beside(k, query_grads), slots[i])
    queries = jnp.concatenate([own, before[1]], axis=0)
    received = jnp.concatenate([before[2], before[3]], axis=0)
    for step in steps[-3::-1]:
        queries = jnp.concatenate([queries, received], axis=0)
        received = swap(beside({steps[1]: 1, steps[0]: None}.get(step), queries), step)
        slots = slots + [slot ^ step for slot in slots]
    flat = pl.pallas_call(
        functools.partial(invert_kernel, rank, train_inputs.shape[0] * n),
        out_shape=jax.ShapeDtypeStruct((rank // 2, 2 * rank), jnp.float32),
        in_specs=[pl.BlockSpec(memory_space=pltpu.VMEM)] * 3,
        out_specs=pl.BlockSpec(memory_space=pltpu.VMEM),
        scratch_shapes=[pltpu.VMEM((rank, 2 * rank), jnp.float32)],
        compiler_params=pltpu.CompilerParams(vmem_limit_bytes=8 * MIB),
        cost_estimate=pl.CostEstimate(flops=10 ** 11, bytes_accessed=10 ** 5, transcendentals=0),
        name="invert",
    )(moment, moment_far, example)
    count = query_grads.shape[0] * n
    return pl.pallas_call(
        functools.partial(score_kernel, rank, slots),
        out_shape=jax.ShapeDtypeStruct((1, count), jnp.float32),
        in_specs=[pl.BlockSpec(memory_space=pltpu.VMEM)] * 3,
        out_specs=pl.BlockSpec(memory_space=pltpu.VMEM),
        scratch_shapes=[pltpu.VMEM((count, 2 * rank), jnp.float32)],
        compiler_params=pltpu.CompilerParams(vmem_limit_bytes=24 * MIB),
        name="score",
    )(flat, queries, received)


def solution(mesh):
    n = mesh.shape["dp"]
    return jax.shard_map(
        functools.partial(body, n),
        mesh=mesh,
        in_specs=(
            P(("groups", "dp"), None),
            P(("groups", "dp"), None),
            P(),
            P(),
            P(("groups", "dp"), None),
        ),
        out_specs=P(("groups", "dp"), None),
        check_vma=False,
    )
```

```python
import functools
import math

import jax
import jax.numpy as jnp
from jax import lax
from jax.experimental import pallas as pl
from jax.experimental.pallas import tpu as pltpu
from jax.sharding import PartitionSpec as P

SEQ = 256
DAMPING = 0.1
CHUNK = 2048
PROJECT_MIB = 53.6
MIB = 1024 * 1024
HIGHEST = lax.Precision.HIGHEST


def project_kernel(rank, chunk, x_hbm, g_hbm, pin_hbm, pout_hbm, m_ref, e_ref, xt, gt, wi, wo, sems):
    x_count, g_count = xt.shape[0], gt.shape[0]

    def copies(src, dst, w_src, w_dst, base, k):
        part = pl.ds(pl.multiple_of(k * chunk, chunk), chunk)
        return (
            pltpu.make_async_copy(w_src.at[:, part], w_dst.at[k], sems.at[0, base + k]),
            pltpu.make_async_copy(src.at[:, part], dst.at[k], sems.at[1, base + k]),
        )

    x_copies = functools.partial(copies, x_hbm, xt, pin_hbm, wi, 0)
    g_copies = functools.partial(copies, g_hbm, gt, pout_hbm, wo, x_count)

    def start(make, k, carry):
        for copy in make(k):
            copy.start()
        return carry

    lax.fori_loop(0, x_count, functools.partial(start, x_copies), 0)
    lax.fori_loop(0, g_count, functools.partial(start, g_copies), 0)

    def multiply(make, tokens, weights, k, total):
        for copy in make(k):
            copy.wait()
        return total + lax.dot_general(
            weights[k], tokens[k], (((1,), (1,)), ((), ())), preferred_element_type=jnp.float32
        )

    zero = jnp.zeros((rank, xt.shape[1]), jnp.float32)
    x_low = lax.fori_loop(0, x_count, functools.partial(multiply, x_copies, xt, wi), zero)
    g_low = lax.fori_loop(0, g_count, functools.partial(multiply, g_copies, gt, wo), zero)
    a0, a1, a2 = split(jnp.concatenate([x_low, g_low], axis=0), 3)
    gram = lax.dot_general(
        jnp.concatenate([a0, a0, a1, a1, a0, a2], axis=1),
        jnp.concatenate([a0, a1, a0, a1, a2, a0], axis=1),
        (((1,), (1,)), ((), ())),
        preferred_element_type=jnp.float32,
    )
    lane = lax.broadcasted_iota(jnp.int32, (rank, 2 * rank), 1)
    m_ref[...] = jnp.where(lane < rank, gram[:rank], gram[rank:])
    e_ref[...] = gram[rank:]


def project(x, g, proj_in, proj_out):
    rank, rows = proj_in.shape[0], x.shape[0]
    chunk = math.gcd(math.gcd(x.shape[1], g.shape[1]), CHUNK)
    x_count, g_count = x.shape[1] // chunk, g.shape[1] // chunk
    out = jax.ShapeDtypeStruct((rank, 2 * rank), jnp.float32)
    return pl.pallas_call(
        functools.partial(project_kernel, rank, chunk),
        out_shape=(out, out),
        in_specs=[pl.BlockSpec(memory_space=pltpu.HBM)] * 4,
        out_specs=(pl.BlockSpec(memory_space=pltpu.VMEM),) * 2,
        scratch_shapes=[
            pltpu.VMEM((x_count, rows, chunk), x.dtype),
            pltpu.VMEM((g_count, rows, chunk), x.dtype),
            pltpu.VMEM((x_count, rank, chunk), x.dtype),
            pltpu.VMEM((g_count, rank, chunk), x.dtype),
            pltpu.SemaphoreType.DMA((2, x_count + g_count)),
        ],
        compiler_params=pltpu.CompilerParams(vmem_limit_bytes=int(PROJECT_MIB * MIB)),
        cost_estimate=pl.CostEstimate(
            flops=2 * rows * rank * (x.shape[1] + g.shape[1]),
            bytes_accessed=2 * (rows + rank) * (x.shape[1] + g.shape[1]),
            transcendentals=0,
        ),
        name="project",
    )(x, g, proj_in, proj_out)


def newton_scales(rank):
    low = 2.0 / (2.0 + rank / DAMPING)
    scales = []
    while 1.0 - low > 0.02:
        image = low * (2.0 - low)
        scale = 2.0 / (1.0 + image)
        scales.append(scale)
        low = scale * image
    return scales


def split(a, terms):
    parts = []
    for _ in range(terms):
        part = a.astype(jnp.bfloat16)
        parts.append(part)
        a = a - part.astype(jnp.float32)
    return parts


def dot(a, b):
    (a0, a1, a2), (b0, b1, b2) = split(a, 3), split(b, 3)
    left = jnp.concatenate([a0, a0, a1, a1, a0, a2], axis=1)
    right = jnp.concatenate([b0, b1, b0, b1, b2, b0], axis=0)
    return jnp.dot(left, right, preferred_element_type=jnp.float32)


def coarse_dot(a, b):
    (a0, a1), (b0, b1) = split(a, 2), split(b, 2)
    left = jnp.concatenate([a0, a1, a0], axis=1)
    right = jnp.concatenate([b0, b0, b1], axis=0)
    return jnp.dot(left, right, preferred_element_type=jnp.float32)


def invert_kernel(rank, tokens, m_ref, mr_ref, e_ref, flat_ref, rows_scr):
    size = 2 * rank
    low = lax.broadcasted_iota(jnp.int32, (rank, size), 1) < rank
    row = lax.broadcasted_iota(jnp.int32, (rank, size), 0)
    col = lax.broadcasted_iota(jnp.int32, (rank, size), 1)
    on_diagonal = jnp.where(low, col, col - rank) == row
    eye = jnp.where(on_diagonal, 1.0, 0.0)

    def blocks(pair):
        zero = jnp.zeros_like(pair)
        return jnp.concatenate([jnp.where(low, pair, zero), jnp.where(low, zero, pair)], axis=0)

    moment = (m_ref[...] + mr_ref[...]) * (1.0 / tokens)
    by_col = jnp.sum(jnp.where(on_diagonal, moment, 0.0), axis=0, keepdims=True)
    half = lax.broadcasted_iota(jnp.int32, (1, size), 1) < rank
    trace_in = jnp.sum(jnp.where(half, by_col, 0.0), axis=1, keepdims=True)
    trace_out = jnp.sum(jnp.where(half, 0.0, by_col), axis=1, keepdims=True)
    damp = jnp.where(half, trace_in, trace_out) * (DAMPING / rank)
    a = moment + eye * damp
    first = (2.0 / (2.0 + rank / DAMPING)) / damp
    t = a * first
    for step, scale in enumerate(newton_scales(rank)):
        turn = scale * (2.0 * eye - t)
        if step == 0:
            x, t = turn * first, coarse_dot(t, blocks(turn))
        else:
            both = coarse_dot(jnp.concatenate([x, t], axis=0), blocks(turn))
            x, t = both[:rank], both[rank:]
    for _ in range(2):
        x = x + coarse_dot(x, blocks(eye - dot(a, blocks(x))))
    inverses = blocks(x)
    example = jnp.where(low, e_ref[...], 0.0)
    left = dot(inverses[rank:], jnp.concatenate([jnp.zeros_like(example), example], axis=0))
    rows_scr[...] = dot(left, jnp.concatenate([inverses[:rank], jnp.zeros_like(example)], axis=0))
    even = rows_scr[pl.ds(0, rank // 2, stride=2), :]
    odd = rows_scr[pl.ds(1, rank // 2, stride=2), :]
    lane = lax.broadcasted_iota(jnp.int32, (rank // 2, size), 1)
    flat_ref[...] = jnp.where(lane < rank, even, pltpu.roll(odd, rank, 1))


def score_kernel(rank, slots, flat_ref, qa_ref, qb_ref, o_ref, acc_scr):
    size = 2 * rank
    me = lax.axis_index("dp")
    count = qa_ref.shape[0] // 16
    each = qa_ref.shape[0] * 2 // len(slots)
    for part, q_ref in enumerate((qa_ref, qb_ref)):
        for i in range(count):
            acc = jnp.zeros((16, size), jnp.float32)
            for j in range(rank // 2):
                block = q_ref[pl.ds(16 * i, 16), pl.ds(j * size, size)].astype(jnp.float32)
                acc = acc + block * flat_ref[j:j + 1, :]
            for h in range(2):
                slot = slots[part * 2 * count + 2 * i + h]
                acc_scr[pl.ds(pl.multiple_of((me ^ slot) * each, each), each), :] = acc[8 * h:8 * h + 8]
    ones = jnp.ones((8, size), jnp.bfloat16)
    sums = sum(
        lax.dot_general(ones, part, (((1,), (1,)), ((), ())), preferred_element_type=jnp.float32)
        for part in split(acc_scr[...], 3)
    )
    o_ref[...] = sums[0:1] * (1.0 / rank)


def body(n, train_inputs, train_grads, proj_in, proj_out, query_grads):
    rank = proj_in.shape[0]
    steps = [1 << b for b in range(n.bit_length() - 1)]

    def swap(value, step):
        return lax.ppermute(value, "dp", [(i, i ^ step) for i in range(n)])

    moment, example = project(train_inputs, train_grads, proj_in, proj_out)
    far, near = steps[-1], steps[-2]
    slots = [0, far, near, far ^ near]
    before = {i: swap(query_grads, slots[i]) for i in (1, 3)}
    first = 1
    moment, before[first], own = lax.optimization_barrier((moment, before[first], query_grads))
    sums, order = [moment], steps
    for step in order[:-1]:
        sums.append(sums[-1] + swap(sums[-1], step))
    moment, moment_far = sums[-1], swap(sums[-1], order[-1])

    def beside(k, value):
        return value if k is None else lax.optimization_barrier((sums[k], value))[1]

    for i, k in ((2, 0),):
        before[i] = swap(beside(k, query_grads), slots[i])
    near_half = jnp.concatenate([own, before[1]], axis=0)
    far_half = jnp.concatenate([before[2], before[3]], axis=0)
    for step in steps[-3:1:-1]:
        near_half, far_half = jnp.concatenate([near_half, far_half], axis=0), jnp.concatenate(
            [swap(near_half, step), swap(far_half, step)], axis=0
        )
        slots = slots + [slot ^ step for slot in slots]
    halves = (near_half, far_half, swap(beside(0, near_half), steps[1]), swap(beside(1, far_half), steps[1]))
    queries = jnp.concatenate(halves, axis=0)
    received = swap(queries, steps[0])
    for step in steps[1::-1]:
        slots = slots + [slot ^ step for slot in slots]
    flat = pl.pallas_call(
        functools.partial(invert_kernel, rank, train_inputs.shape[0] * n),
        out_shape=jax.ShapeDtypeStruct((rank // 2, 2 * rank), jnp.float32),
        in_specs=[pl.BlockSpec(memory_space=pltpu.VMEM)] * 3,
        out_specs=pl.BlockSpec(memory_space=pltpu.VMEM),
        scratch_shapes=[pltpu.VMEM((rank, 2 * rank), jnp.float32)],
        compiler_params=pltpu.CompilerParams(vmem_limit_bytes=8 * MIB),
        cost_estimate=pl.CostEstimate(flops=10 ** 11, bytes_accessed=10 ** 5, transcendentals=0),
        name="invert",
    )(moment, moment_far, example)
    count = query_grads.shape[0] * n
    return pl.pallas_call(
        functools.partial(score_kernel, rank, slots),
        out_shape=jax.ShapeDtypeStruct((1, count), jnp.float32),
        in_specs=[pl.BlockSpec(memory_space=pltpu.VMEM)] * 3,
        out_specs=pl.BlockSpec(memory_space=pltpu.VMEM),
        scratch_shapes=[pltpu.VMEM((count, 2 * rank), jnp.float32)],
        compiler_params=pltpu.CompilerParams(vmem_limit_bytes=24 * MIB),
        name="score",
    )(flat, queries, received)


def solution(mesh):
    n = mesh.shape["dp"]
    return jax.shard_map(
        functools.partial(body, n),
        mesh=mesh,
        in_specs=(
            P(("groups", "dp"), None),
            P(("groups", "dp"), None),
            P(),
            P(),
            P(("groups", "dp"), None),
        ),
        out_specs=P(("groups", "dp"), None),
        check_vma=False,
    )
```
